32 devices in a mesh: dp: 8 (over y, x, core), tensor: 4 (over z).
Axes of the slice: x: 2, y: 2, z: 4, core: 2. Of those that a mesh axis runs over, the one named last changes fastest.
Arguments:
- hidden: bfloat16 [2048, 4608], P('dp', 'tensor'), may hold values from -0.890625 to 0.890625
- out_grad: bfloat16 [2048, 2304], P('dp'), may hold values from -1.1875 to 1.1875
- weight: bfloat16 [4608, 2304], P('tensor'), may hold values from -0.09375 to 0.09375
- first_moment: float32 [2304, 4608], P('dp', 'tensor'), may hold values from -3 to 3
- second_moment: float32 [2304, 4608], P('dp', 'tensor'), may hold values from 0.1 to 4
- next_hidden: bfloat16 [2048, 4608], P('dp', 'tensor'), may hold values from -6 to 6
Outputs:
- input_grad: bfloat16 [2048, 4608], P('dp', 'tensor')
- first_new: float32 [2304, 4608], P('dp', 'tensor')
- second_new: float32 [2304, 4608], P('dp', 'tensor')
- new_weight: bfloat16 [2304, 4608], P('dp', 'tensor')
- next_out: bfloat16 [2048, 2304], P('dp')
The draws below stay inside these ranges and needn't reach their ends.
All inputs are finite; a program needn't handle non-finite values.
Results may differ from the reference program's by a relative error of at most 0.007.
Values may be sent and summed in bfloat16 or wider, within the bound.
A program may use at most 128 MiB of HBM per device.

```python
import math
import jax
import jax.numpy as jnp

D = 2304
FF = 4608
TOKENS = 2048


def strengthened(entries, rng, source, target, parts, factor):
    owner, partner = [(jnp.arange(entries.shape[position]) // (entries.shape[position] // parts)).reshape([-1 if axis == position else 1 for axis in range(entries.ndim)]) for position in (source, target)]
    chosen = jax.random.permutation(rng, parts)[partner]
    strong = (owner == chosen) | (owner == (partner + parts // 2) % parts)
    return jnp.where(strong, factor * entries, entries)


def levels(key, dims, pieces, least, high):
    level = 1.0
    for position, parts in pieces:
        steps = jax.random.uniform(jax.random.fold_in(jax.random.fold_in(key, 6), position), (parts,), jnp.float32, least / len(pieces), high / len(pieces))
        level = level * jnp.repeat(jnp.exp(steps), dims[position] // parts).reshape((-1,) + (1,) * (len(dims) - 1 - position))
    return level


def normal_values(key, shape, scale, most, shards=(), dtype=jnp.bfloat16):
    result = scale * jax.random.normal(key, shape, jnp.float32)
    if shards:
        result = result * levels(key, shape, shards, -0.22, 0.18)
    return jnp.clip(result, -most, most).astype(dtype)


def gaussian_with(stream_key, extent, width, limit, split, heavy, held_as=jnp.bfloat16):
    drawn = width * jax.random.normal(stream_key, extent, jnp.float32)
    if split:
        drawn = drawn * levels(stream_key, extent, split, -0.22, 0.18)
    return jnp.clip(strengthened(drawn, jax.random.fold_in(stream_key, 3), *heavy), -limit, limit).astype(held_as)


def setup_inputs(seed: int = 0) -> dict:
    keys = jax.random.split(jax.random.key(seed), 7)
    return {
        "hidden": normal_values(keys[0], (TOKENS, FF), (TOKENS ** -0.25), 0.890625, ((0, 8), (1, 4))),
        "out_grad": gaussian_with(keys[1], (TOKENS, D), (TOKENS ** -0.25), 1.1875, ((0, 8),), (0, 1, 8, 2.0)),
        "weight": normal_values(keys[2], (FF, D), FF ** -0.5, 0.09375, ((0, 4),)),
        "first_moment": normal_values(keys[3], (D, FF), 0.5, 3.0, ((0, 8), (1, 4)), jnp.float32),
        "second_moment": jnp.clip(jnp.exp(math.log(4.0) - 3.6888794 * jax.random.uniform(keys[4], (D, FF), jnp.float32) ** levels(keys[4], (D, FF), ((0, 8), (1, 4)), -0.2, 0.2)), 0.1, 4.0),
        "next_hidden": normal_values(keys[5], (TOKENS, FF), 1.0, 6.0, ((0, 8), (1, 4))),
    }


beta_first = 0.9
beta_second = 0.95
learn_rate = 0.001
weight_decay = 0.1
epsilon = 1e-08
correct_first = 0.999973438601112
correct_second = 0.99407947077967

def reference(hidden, out_grad, weight, first_moment, second_moment, next_hidden):
    input_grad = jnp.dot(out_grad, weight.T, preferred_element_type=jnp.float32).astype(jnp.bfloat16)
    grad = jnp.dot(out_grad.T, hidden, preferred_element_type=jnp.float32)
    first_new = beta_first * first_moment + (1.0 - beta_first) * grad
    second_new = beta_second * second_moment + (1.0 - beta_second) * grad * grad
    current = weight.T.astype(jnp.float32)
    update = first_new / correct_first / (jnp.sqrt(second_new / correct_second) + epsilon)
    new_weight = (current - learn_rate * (update + weight_decay * current)).astype(jnp.bfloat16)
    next_out = jnp.dot(next_hidden, new_weight.T, preferred_element_type=jnp.float32).astype(jnp.bfloat16)
    return (input_grad, first_new, second_new, new_weight, next_out)
```

```python
import functools

import jax
import jax.numpy as jnp
from jax import lax
from jax.experimental import pallas as pl
from jax.experimental.pallas import tpu as pltpu
from jax.sharding import PartitionSpec as P

MESH = pl.DeviceIdType.MESH

beta_first = 0.9
beta_second = 0.95
learn_rate = 0.001
weight_decay = 0.1
epsilon = 1e-08
correct_first = 0.999973438601112
correct_second = 0.99407947077967


def adam(first_moment, second_moment, grad):
    first_new = beta_first * first_moment + (1.0 - beta_first) * grad
    second_new = beta_second * second_moment + (1.0 - beta_second) * grad * grad
    return first_new, second_new


def kernel(
    n, m, chunks,
    og_t, hidden, out_grad_hbm, weight_hbm, current_hbm, first_hbm, second_hbm, next_hidden_hbm,
    grad_out, input_grad, new_weight, next_out,
    out_grad, weight, current, first, second, next_hidden,
    parts, whole, partial, inward, from_out, *rest,
):
    bits = n.bit_length() - 1
    landed = rest[:bits]
    (load_sem, rs_send, rs_recv, ag_send, ag_recv,
     in_send, a_recv, b_recv, out_send) = rest[bits:]
    half = m // 2
    rows = first.shape[0]
    rc = rows // chunks
    width = hidden.shape[1]
    me = lax.axis_index("dp")
    at = lax.axis_index("tensor")
    mine = [(me // (1 << b)) % 2 for b in range(bits)]
    partner = [me + (1 << b) * (1 - 2 * mine[b]) for b in range(bits)]
    left = at < half
    depth = jnp.where(left, half - 1 - at, at - half)
    inner = jnp.where(left, at + 1, at - 1)
    outer = jnp.where(left, at - 1, at + 1)
    has_outer = depth < half - 1

    loads = [
        pltpu.make_async_copy(src, dst, load_sem.at[i])
        for i, (src, dst) in enumerate((
            (first_hbm, first), (second_hbm, second), (current_hbm, current),
            (next_hidden_hbm, next_hidden), (out_grad_hbm, out_grad), (weight_hbm, weight),
        ))
    ]
    for load in loads:
        load.start()

    barrier = pltpu.get_barrier_semaphore()
    for b in range(bits):
        pl.semaphore_signal(barrier, inc=1, device_id={"dp": partner[b]}, device_id_type=MESH)
    pl.semaphore_signal(barrier, inc=1, device_id={"tensor": inner}, device_id_type=MESH)

    @pl.when(has_outer)
    def _():
        pl.semaphore_signal(barrier, inc=1, device_id={"tensor": outer}, device_id_type=MESH)

    pl.semaphore_wait(barrier, bits + 1 + jnp.where(has_outer, 1, 0))

    def order(c):
        high = list(range(1, bits))
        return [0] + (high if c % 2 == 0 else high[::-1])

    def region(c, fixed):
        return (c,) + tuple(fixed.get(b, slice(None)) for b in reversed(range(bits)))

    def rs_copy(c, k):
        o = order(c)
        fixed = {b: mine[b] for b in o[:k]}
        fixed[o[k]] = 1 - mine[o[k]]
        return pltpu.make_async_remote_copy(
            src_ref=parts.at[region(c, fixed)],
            dst_ref=landed[k].at[c],
            send_sem=rs_send.at[c, k],
            recv_sem=rs_recv.at[c, k],
            device_id={"dp": partner[o[k]]},
            device_id_type=MESH,
        )

    def ag_copy(c, j):
        o = order(c)
        k = bits - 1 - j
        fixed = {b: mine[b] for b in o[: k + 1]}
        return pltpu.make_async_remote_copy(
            src_ref=whole.at[region(c, fixed)],
            dst_ref=whole.at[region(c, fixed)],
            send_sem=ag_send.at[c, j],
            recv_sem=ag_recv.at[c, j],
            device_id={"dp": partner[o[k]]},
            device_id_type=MESH,
        )

    def in_copy(c, middle):
        return pltpu.make_async_remote_copy(
            src_ref=inward.at[c],
            dst_ref=(next_out if middle else from_out).at[c],
            send_sem=in_send.at[c],
            recv_sem=(b_recv if middle else a_recv).at[c],
            device_id={"tensor": inner},
            device_id_type=MESH,
        )

    def out_copy(c):
        return pltpu.make_async_remote_copy(
            src_ref=next_out.at[c],
            dst_ref=next_out.at[c],
            send_sem=out_send.at[c],
            recv_sem=b_recv.at[c],
            device_id={"tensor": outer},
            device_id_type=MESH,
        )

    def send_inward(c):
        if half == 1:
            in_copy(c, True).start()
        else:
            @pl.when(depth > 0)
            def _():
                in_copy(c, False).start()

            @pl.when(depth == 0)
            def _():
                in_copy(c, True).start()

    def stage(c, s):
        o = order(c)
        if s == 0:
            lhs = jnp.concatenate(
                [og_t[q * rows + c * rc : q * rows + (c + 1) * rc, :] for q in range(n)], axis=0
            )
            part = jnp.dot(lhs, hidden[...], preferred_element_type=jnp.float32)
            parts[c] = part.astype(jnp.bfloat16).reshape((2,) * bits + (rc, width))
            rs_copy(c, 0).start()
        elif s < bits:
            rs_copy(c, s - 1).wait_recv()
            keep = region(c, {b: mine[b] for b in o[:s]})
            parts[keep] = (
                parts[keep].astype(jnp.float32) + landed[s - 1][c].astype(jnp.float32)
            ).astype(jnp.bfloat16)
            rs_copy(c, s).start()
        elif s == bits:
            rs_copy(c, bits - 1).wait_recv()
            own = region(c, dict(enumerate(mine)))
            grad = (
                parts[own].astype(jnp.float32) + landed[bits - 1][c].astype(jnp.float32)
            ).astype(jnp.bfloat16)
            span = slice(c * rc, (c + 1) * rc)
            grad_out[span, :] = grad
            first_new, second_new = adam(first[span, :], second[span, :], grad.astype(jnp.float32))
            update = first_new * (1.0 / correct_first) / (
                jnp.sqrt(second_new * (1.0 / correct_second)) + epsilon
            )
            now = current[span, :].astype(jnp.float32)
            result = (now - learn_rate * (update + weight_decay * now)).astype(jnp.bfloat16)
            new_weight[span, :] = result
            whole[own] = result
            ag_copy(c, 0).start()
        elif s < 2 * bits:
            ag_copy(c, s - bits - 1).wait_recv()
            ag_copy(c, s - bits).start()
        elif s == 2 * bits:
            ag_copy(c, bits - 1).wait_recv()
            product = lax.dot_general(
                whole[c].reshape((n * rc, width)), next_hidden[...],
                (((1,), (1,)), ((), ())), preferred_element_type=jnp.float32,
            )
            partial[c] = product

            @pl.when(jnp.logical_not(has_outer))
            def _():
                inward[c] = product.astype(jnp.bfloat16)
                send_inward(c)
        elif s == 2 * bits + 1:
            @pl.when(has_outer)
            def _():
                in_copy(c, False).wait_recv()
                inward[c] = (partial[c] + from_out[c].astype(jnp.float32)).astype(jnp.bfloat16)
                send_inward(c)
        else:
            out_copy(c).wait_recv()

            @pl.when(depth == 0)
            def _():
                next_out[c] = (
                    inward[c].astype(jnp.float32) + next_out[c].astype(jnp.float32)
                ).astype(jnp.bfloat16)

            @pl.when(has_outer)
            def _():
                out_copy(c).start()

    pieces = 3
    cut = width // pieces
    last = 2 * bits + 2
    for t in range(chunks + last):
        for c in range(chunks):
            if 0 <= t - c <= last:
                if t - c == bits and c == 0:
                    for load in loads[:3]:
                        load.wait()
                if t - c == 2 * bits and c == 0:
                    loads[3].wait()
                stage(c, t - c)
        if 1 <= t <= pieces:
            if t == 1:
                loads[4].wait()
                loads[5].wait()
            span = slice((t - 1) * cut, t * cut)
            input_grad[:, span] = lax.dot_general(
                out_grad[...], weight[span, :], (((1,), (1,)), ((), ())),
                preferred_element_type=jnp.float32,
            ).astype(jnp.bfloat16)

    for c in range(chunks):
        for k in range(bits):
            rs_copy(c, k).wait_send()
            ag_copy(c, k).wait_send()
        in_copy(c, False).wait_send()

        @pl.when(has_outer)
        def _():
            out_copy(c).wait_send()


def solution(mesh):
    n, m = mesh.shape["dp"], mesh.shape["tensor"]
    bits = n.bit_length() - 1

    def shards(hidden, out_grad, weight, first_moment, second_moment, next_hidden):
        tokens, width = hidden.shape
        rows = first_moment.shape[0]
        features = out_grad.shape[1]
        rc = 48
        chunks = rows // rc
        cube = (2,) * bits
        position = lax.axis_index("dp") * rows
        current = lax.dynamic_slice_in_dim(weight, position, rows, 1).T
        vmem = pl.BlockSpec(memory_space=pltpu.VMEM)
        hbm = pl.BlockSpec(memory_space=pl.ANY)
        bf16, f32 = jnp.bfloat16, jnp.float32
        dma = pltpu.SemaphoreType.DMA
        grad, input_grad, new_weight, next_out = pl.pallas_call(
            functools.partial(kernel, n, m, chunks),
            out_shape=(
                jax.ShapeDtypeStruct((rows, width), bf16),
                jax.ShapeDtypeStruct((tokens, width), bf16),
                jax.ShapeDtypeStruct((rows, width), bf16),
                jax.ShapeDtypeStruct((chunks, n * rc, tokens), bf16),
            ),
            in_specs=[vmem] * 2 + [hbm] * 6,
            out_specs=[vmem] * 4,
            scratch_shapes=[
                pltpu.VMEM(out_grad.shape, bf16),
                pltpu.VMEM(weight.shape, bf16),
                pltpu.VMEM((rows, width), bf16),
                pltpu.VMEM((rows, width), f32),
                pltpu.VMEM((rows, width), f32),
                pltpu.VMEM(next_hidden.shape, bf16),
                pltpu.VMEM((chunks,) + cube + (rc, width), bf16),
                pltpu.VMEM((chunks,) + cube + (rc, width), bf16),
                pltpu.VMEM((chunks, n * rc, tokens), f32),
                pltpu.VMEM((chunks, n * rc, tokens), bf16),
                pltpu.VMEM((chunks, n * rc, tokens), bf16),
            ]
            + [
                pltpu.VMEM((chunks,) + (2,) * (bits - 1 - k) + (rc, width), bf16)
                for k in range(bits)
            ]
            + [
                dma((6,)),
                dma((chunks, bits)), dma((chunks, bits)),
                dma((chunks, bits)), dma((chunks, bits)),
                dma((chunks,)), dma((chunks,)), dma((chunks,)), dma((chunks,)),
            ],
            compiler_params=pltpu.CompilerParams(
                collective_id=0, has_side_effects=True, vmem_limit_bytes=56 * 1024 * 1024
            ),
            cost_estimate=pl.CostEstimate(
                flops=6 * tokens * width * features,
                bytes_accessed=16 * 1024 * 1024,
                transcendentals=rows * width,
            ),
        )(out_grad.T, hidden, out_grad, weight, current, first_moment, second_moment, next_hidden)
        first_new, second_new = adam(first_moment, second_moment, grad.astype(f32))
        next_out = (
            next_out.reshape(chunks, n, rc, tokens).transpose(3, 1, 0, 2).reshape(tokens, features)
        )
        return input_grad, first_new, second_new, new_weight, next_out

    placed = (
        P("dp", "tensor"),
        P("dp", None),
        P("tensor", None),
        P("dp", "tensor"),
        P("dp", "tensor"),
        P("dp", "tensor"),
    )
    return jax.shard_map(
        shards,
        mesh=mesh,
        in_specs=placed,
        out_specs=(
            P("dp", "tensor"),
            P("dp", "tensor"),
            P("dp", "tensor"),
            P("dp", "tensor"),
            P("dp", None),
        ),
        check_vma=False,
    )
```

```python
import functools
import math

import jax
import jax.numpy as jnp
from jax import lax
from jax.experimental import pallas as pl
from jax.experimental.pallas import tpu as pltpu
from jax.sharding import PartitionSpec as P

MESH = pl.DeviceIdType.MESH

beta_first = 0.9
beta_second = 0.95
learn_rate = 0.001
weight_decay = 0.1
epsilon = 1e-08
correct_first = 0.999973438601112
correct_second = 0.99407947077967


def adam(first_moment, second_moment, grad):
    first_new = beta_first * first_moment + (1.0 - beta_first) * grad
    second_new = beta_second * second_moment + (1.0 - beta_second) * grad * grad
    return first_new, second_new


def window_size(rows):
    return -(-(rows + 128 - math.gcd(rows, 128)) // 128) * 128


def kernel(
    n, m, chunks, lag,
    out_grad, hidden, weight_hbm, first_hbm, second_hbm, next_hidden_hbm,
    grad_out, input_grad, new_weight, next_out,
    og_t, weight, current, first, second, next_hidden,
    parts, whole, partial, inward, from_out, *rest,
):
    bits = n.bit_length() - 1
    landed = rest[:bits]
    (load_sem, rs_send, rs_recv, ag_send, ag_recv,
     in_send, a_recv, b_recv, out_send) = rest[bits:]
    half = m // 2
    rows = first.shape[0]
    rc = rows // chunks
    group = 3 if chunks % 3 == 0 else 1
    width = hidden.shape[1]
    me = lax.axis_index("dp")
    at = lax.axis_index("tensor")
    mine = [(me // (1 << b)) % 2 for b in range(bits)]
    partner = [me + (1 << b) * (1 - 2 * mine[b]) for b in range(bits)]
    left = at < half
    depth = jnp.where(left, half - 1 - at, at - half)
    inner = jnp.where(left, at + 1, at - 1)
    outer = jnp.where(left, at - 1, at + 1)
    has_outer = depth < half - 1

    loads = [
        pltpu.make_async_copy(src, dst, load_sem.at[i])
        for i, (src, dst) in enumerate((
            (weight_hbm, weight), (first_hbm, first), (second_hbm, second),
            (next_hidden_hbm, next_hidden),
        ))
    ]
    for load in loads:
        load.start()

    barrier = pltpu.get_barrier_semaphore()
    for b in range(bits):
        pl.semaphore_signal(barrier, inc=1, device_id={"dp": partner[b]}, device_id_type=MESH)
    pl.semaphore_signal(barrier, inc=1, device_id={"tensor": inner}, device_id_type=MESH)

    @pl.when(has_outer)
    def _():
        pl.semaphore_signal(barrier, inc=1, device_id={"tensor": outer}, device_id_type=MESH)

    og_t[...] = out_grad[...].T
    pl.semaphore_wait(barrier, bits + 1 + jnp.where(has_outer, 1, 0))

    def order(c):
        high = list(range(1, bits))
        return [0] + (high if c % 2 == 0 else high[::-1])

    def region(c, fixed):
        return (c,) + tuple(fixed.get(b, slice(None)) for b in reversed(range(bits)))

    def rs_copy(c, k):
        o = order(c)
        fixed = {b: mine[b] for b in o[:k]}
        fixed[o[k]] = 1 - mine[o[k]]
        return pltpu.make_async_remote_copy(
            src_ref=parts.at[region(c, fixed)],
            dst_ref=landed[k].at[c],
            send_sem=rs_send.at[c, k],
            recv_sem=rs_recv.at[c, k],
            device_id={"dp": partner[o[k]]},
            device_id_type=MESH,
        )

    def ag_copy(c, j):
        o = order(c)
        k = bits - 1 - j
        fixed = {b: mine[b] for b in o[: k + 1]}
        return pltpu.make_async_remote_copy(
            src_ref=whole.at[region(c, fixed)],
            dst_ref=whole.at[region(c, fixed)],
            send_sem=ag_send.at[c, j],
            recv_sem=ag_recv.at[c, j],
            device_id={"dp": partner[o[k]]},
            device_id_type=MESH,
        )

    def in_copy(c, middle):
        return pltpu.make_async_remote_copy(
            src_ref=inward.at[c],
            dst_ref=next_out.at[:, c] if middle else from_out.at[c],
            send_sem=in_send.at[c],
            recv_sem=(b_recv if middle else a_recv).at[c],
            device_id={"tensor": inner},
            device_id_type=MESH,
        )

    def out_copy(c):
        return pltpu.make_async_remote_copy(
            src_ref=next_out.at[:, c],
            dst_ref=next_out.at[:, c],
            send_sem=out_send.at[c],
            recv_sem=b_recv.at[c],
            device_id={"tensor": outer},
            device_id_type=MESH,
        )

    def send_inward(c):
        if half == 1:
            in_copy(c, True).start()
        else:
            @pl.when(depth > 0)
            def _():
                in_copy(c, False).start()

            @pl.when(depth == 0)
            def _():
                in_copy(c, True).start()

    def stage(c, s):
        o = order(c)
        if s == 0:
            if c % group == 0:
                lhs = jnp.concatenate(
                    [
                        og_t[q * rows + d * rc : q * rows + (d + 1) * rc, :]
                        for d in range(c, c + group) for q in range(n)
                    ],
                    axis=0,
                )
                part = jnp.dot(lhs, hidden[...], preferred_element_type=jnp.float32)
                parts[c : c + group] = part.astype(jnp.bfloat16).reshape(
                    (group,) + (2,) * bits + (rc, width)
                )
            rs_copy(c, 0).start()
        elif s < bits:
            rs_copy(c, s - 1).wait_recv()
            keep = region(c, {b: mine[b] for b in o[:s]})
            parts[keep] = (
                parts[keep].astype(jnp.float32) + landed[s - 1][c].astype(jnp.float32)
            ).astype(jnp.bfloat16)
            rs_copy(c, s).start()
        elif s == bits:
            rs_copy(c, bits - 1).wait_recv()
            own = region(c, dict(enumerate(mine)))
            grad = (
                parts[own].astype(jnp.float32) + landed[bits - 1][c].astype(jnp.float32)
            ).astype(jnp.bfloat16)
            span = slice(c * rc, (c + 1) * rc)
            grad_out[span, :] = grad
            first_new, second_new = adam(first[span, :], second[span, :], grad.astype(jnp.float32))
            update = first_new * (1.0 / correct_first) / (
                jnp.sqrt(second_new * (1.0 / correct_second)) + epsilon
            )
            now = current[span, :]
            result = (now - learn_rate * (update + weight_decay * now)).astype(jnp.bfloat16)
            new_weight[span, :] = result
            whole[own] = result
            ag_copy(c, 0).start()
        elif s < 2 * bits:
            ag_copy(c, s - bits - 1).wait_recv()
            ag_copy(c, s - bits).start()
        elif s == 2 * bits:
            ag_copy(c, bits - 1).wait_recv()
            product = lax.dot_general(
                whole[c].reshape((n * rc, width)), next_hidden[...],
                (((1,), (1,)), ((), ())), preferred_element_type=jnp.float32,
            )
            product = product.reshape((n, rc, product.shape[1]))
            partial[c] = product

            @pl.when(jnp.logical_not(has_outer))
            def _():
                inward[c] = product.astype(jnp.bfloat16)
                send_inward(c)
        elif s == 2 * bits + 1:
            @pl.when(has_outer)
            def _():
                in_copy(c, False).wait_recv()
                inward[c] = (partial[c] + from_out[c].astype(jnp.float32)).astype(jnp.bfloat16)
                send_inward(c)
        else:
            out_copy(c).wait_recv()

            @pl.when(depth == 0)
            def _():
                next_out[:, c] = (
                    inward[c].astype(jnp.float32) + next_out[:, c].astype(jnp.float32)
                ).astype(jnp.bfloat16)

            @pl.when(has_outer)
            def _():
                out_copy(c).start()

    def own_weight():
        span = window_size(rows)
        start = (me * rows) // 128 * 128
        near = weight[:, pl.ds(pl.multiple_of(start, 128), span)]
        shift = me * rows - start
        row = lax.broadcasted_iota(jnp.int32, (rows, span), 0)
        column = lax.broadcasted_iota(jnp.int32, (rows, span), 1)
        pick = jnp.where(column == row + shift, 1.0, 0.0).astype(jnp.bfloat16)
        current[...] = lax.dot_general(
            pick, near, (((1,), (1,)), ((), ())), preferred_element_type=jnp.float32
        )

    pieces = 3
    cut = width // pieces
    last = 2 * bits + 2
    for t in range(chunks + lag * last):
        for s in reversed(range(last + 1)):
            c = t - lag * s
            if 0 <= c < chunks:
                if s == bits and c == 0:
                    loads[1].wait()
                    loads[2].wait()
                if s == 2 * bits and c == 0:
                    loads[3].wait()
                stage(c, s)
        if t == 1:
            loads[0].wait()
            own_weight()
        if t in (4, 6, 8):
            span = slice((t - 4) // 2 * cut, (t - 2) // 2 * cut)
            input_grad[:, span] = lax.dot_general(
                out_grad[...], weight[span, :], (((1,), (1,)), ((), ())),
                preferred_element_type=jnp.float32,
            ).astype(jnp.bfloat16)

    for c in range(chunks):
        for k in range(bits):
            rs_copy(c, k).wait_send()
            ag_copy(c, k).wait_send()
        in_copy(c, False).wait_send()

        @pl.when(has_outer)
        def _():
            out_copy(c).wait_send()


def solution(mesh):
    n, m = mesh.shape["dp"], mesh.shape["tensor"]
    bits = n.bit_length() - 1

    def shards(hidden, out_grad, weight, first_moment, second_moment, next_hidden):
        tokens, width = hidden.shape
        rows = first_moment.shape[0]
        features = out_grad.shape[1]
        rc = 16
        chunks = rows // rc
        cube = (2,) * bits
        vmem = pl.BlockSpec(memory_space=pltpu.VMEM)
        hbm = pl.BlockSpec(memory_space=pl.ANY)
        bf16, f32 = jnp.bfloat16, jnp.float32
        dma = pltpu.SemaphoreType.DMA
        grad, input_grad, new_weight, next_out = pl.pallas_call(
            functools.partial(kernel, n, m, chunks, 3),
            out_shape=(
                jax.ShapeDtypeStruct((rows, width), bf16),
                jax.ShapeDtypeStruct((tokens, width), bf16),
                jax.ShapeDtypeStruct((rows, width), bf16),
                jax.ShapeDtypeStruct((n, chunks, rc, tokens), bf16),
            ),
            in_specs=[vmem] * 2 + [hbm] * 4,
            out_specs=[vmem] * 4,
            scratch_shapes=[
                pltpu.VMEM((features, tokens), bf16),
                pltpu.VMEM(weight.shape, bf16),
                pltpu.VMEM((rows, width), f32),
                pltpu.VMEM((rows, width), f32),
                pltpu.VMEM((rows, width), f32),
                pltpu.VMEM(next_hidden.shape, bf16),
                pltpu.VMEM((chunks,) + cube + (rc, width), bf16),
                pltpu.VMEM((chunks,) + cube + (rc, width), bf16),
                pltpu.VMEM((chunks, n, rc, tokens), f32),
                pltpu.VMEM((chunks, n, rc, tokens), bf16),
                pltpu.VMEM((chunks, n, rc, tokens), bf16),
            ]
            + [
                pltpu.VMEM((chunks,) + (2,) * (bits - 1 - k) + (rc, width), bf16)
                for k in range(bits)
            ]
            + [
                dma((4,)),
                dma((chunks, bits)), dma((chunks, bits)),
                dma((chunks, bits)), dma((chunks, bits)),
                dma((chunks,)), dma((chunks,)), dma((chunks,)), dma((chunks,)),
            ],
            compiler_params=pltpu.CompilerParams(
                collective_id=0, has_side_effects=True, vmem_limit_bytes=56 * 1024 * 1024
            ),
            cost_estimate=pl.CostEstimate(
                flops=6 * tokens * width * features,
                bytes_accessed=16 * 1024 * 1024,
                transcendentals=rows * width,
            ),
        )(out_grad, hidden, weight, first_moment, second_moment, next_hidden)
        first_new, second_new = adam(first_moment, second_moment, grad.astype(f32))
        next_out = next_out.reshape(features, tokens).T
        return input_grad, first_new, second_new, new_weight, next_out

    placed = (
        P("dp", "tensor"),
        P("dp", None),
        P("tensor", None),
        P("dp", "tensor"),
        P("dp", "tensor"),
        P("dp", "tensor"),
    )
    return jax.shard_map(
        shards,
        mesh=mesh,
        in_specs=placed,
        out_specs=(
            P("dp", "tensor"),
            P("dp", "tensor"),
            P("dp", "tensor"),
            P("dp", "tensor"),
            P("dp", None),
        ),
        check_vma=False,
    )
```

```python
import functools
import math

import jax
import jax.numpy as jnp
from jax import lax
from jax.experimental import pallas as pl
from jax.experimental.pallas import tpu as pltpu
from jax.sharding import PartitionSpec as P

MESH = pl.DeviceIdType.MESH

beta_first = 0.9
beta_second = 0.95
learn_rate = 0.001
weight_decay = 0.1
epsilon = 1e-08
correct_first = 0.999973438601112
correct_second = 0.99407947077967


def adam(first_moment, second_moment, grad):
    first_new = beta_first * first_moment + (1.0 - beta_first) * grad
    second_new = beta_second * second_moment + (1.0 - beta_second) * grad * grad
    return first_new, second_new


def window_size(rows):
    return -(-(rows + 128 - math.gcd(rows, 128)) // 128) * 128


def kernel(
    n, m, chunks, lag,
    out_grad, hidden, weight_hbm, first_hbm, second_hbm, next_hidden_hbm,
    grad_out, input_grad, new_weight, next_out,
    og_t, weight, current, first, second, next_hidden, next_t,
    parts, whole, partial, inward, from_out, *rest,
):
    bits = n.bit_length() - 1
    landed = rest[:bits]
    (load_sem, rs_send, rs_recv, ag_send, ag_recv,
     in_send, a_recv, b_recv, out_send) = rest[bits:]
    half = m // 2
    rows = first.shape[0]
    rc = rows // chunks
    group = 3 if chunks % 3 == 0 else 1
    width = hidden.shape[1]
    me = lax.axis_index("dp")
    at = lax.axis_index("tensor")
    mine = [(me // (1 << b)) % 2 for b in range(bits)]
    partner = [me + (1 << b) * (1 - 2 * mine[b]) for b in range(bits)]
    left = at < half
    depth = jnp.where(left, half - 1 - at, at - half)
    inner = jnp.where(left, at + 1, at - 1)
    outer = jnp.where(left, at - 1, at + 1)
    has_outer = depth < half - 1

    loads = [
        pltpu.make_async_copy(src, dst, load_sem.at[i])
        for i, (src, dst) in enumerate((
            (weight_hbm, weight), (first_hbm, first), (second_hbm, second),
            (next_hidden_hbm, next_hidden),
        ))
    ]
    for load in loads:
        load.start()

    barrier = pltpu.get_barrier_semaphore()
    for b in range(bits):
        pl.semaphore_signal(barrier, inc=1, device_id={"dp": partner[b]}, device_id_type=MESH)
    pl.semaphore_signal(barrier, inc=1, device_id={"tensor": inner}, device_id_type=MESH)

    @pl.when(has_outer)
    def _():
        pl.semaphore_signal(barrier, inc=1, device_id={"tensor": outer}, device_id_type=MESH)

    og_t[...] = out_grad[...].T
    pl.semaphore_wait(barrier, bits + 1 + jnp.where(has_outer, 1, 0))

    def order(c):
        high = list(range(1, bits))
        return [0] + (high if c % 2 == 0 else high[::-1])

    def region(c, fixed):
        return (c,) + tuple(fixed.get(b, slice(None)) for b in reversed(range(bits)))

    def rs_copy(c, k):
        o = order(c)
        fixed = {b: mine[b] for b in o[:k]}
        fixed[o[k]] = 1 - mine[o[k]]
        return pltpu.make_async_remote_copy(
            src_ref=parts.at[region(c, fixed)],
            dst_ref=landed[k].at[c],
            send_sem=rs_send.at[c, k],
            recv_sem=rs_recv.at[c, k],
            device_id={"dp": partner[o[k]]},
            device_id_type=MESH,
        )

    def ag_copy(c, j):
        o = order(c)
        k = bits - 1 - j
        fixed = {b: mine[b] for b in o[: k + 1]}
        return pltpu.make_async_remote_copy(
            src_ref=whole.at[region(c, fixed)],
            dst_ref=whole.at[region(c, fixed)],
            send_sem=ag_send.at[c, j],
            recv_sem=ag_recv.at[c, j],
            device_id={"dp": partner[o[k]]},
            device_id_type=MESH,
        )

    def in_copy(c, middle):
        return pltpu.make_async_remote_copy(
            src_ref=inward.at[c],
            dst_ref=next_out.at[:, c] if middle else from_out.at[c],
            send_sem=in_send.at[c],
            recv_sem=(b_recv if middle else a_recv).at[c],
            device_id={"tensor": inner},
            device_id_type=MESH,
        )

    def out_copy(c):
        return pltpu.make_async_remote_copy(
            src_ref=next_out.at[:, c],
            dst_ref=next_out.at[:, c],
            send_sem=out_send.at[c],
            recv_sem=b_recv.at[c],
            device_id={"tensor": outer},
            device_id_type=MESH,
        )

    def send_inward(c):
        if half == 1:
            in_copy(c, True).start()
        else:
            @pl.when(depth > 0)
            def _():
                in_copy(c, False).start()

            @pl.when(depth == 0)
            def _():
                in_copy(c, True).start()

    def stage(c, s):
        o = order(c)
        if s == 0:
            if c % group == 0:
                lhs = jnp.concatenate(
                    [
                        og_t[q * rows + d * rc : q * rows + (d + 1) * rc, :]
                        for d in range(c, c + group) for q in range(n)
                    ],
                    axis=0,
                )
                part = jnp.dot(lhs, hidden[...], preferred_element_type=jnp.float32)
                parts[c : c + group] = part.astype(jnp.bfloat16).reshape(
                    (group,) + (2,) * bits + (rc, width)
                )
            rs_copy(c, 0).start()
        elif s < bits:
            rs_copy(c, s - 1).wait_recv()
            keep = region(c, {b: mine[b] for b in o[:s]})
            parts[keep] = parts[keep] + landed[s - 1][c]
            rs_copy(c, s).start()
        elif s == bits:
            rs_copy(c, bits - 1).wait_recv()
            own = region(c, dict(enumerate(mine)))
            grad = (
                parts[own].astype(jnp.float32) + landed[bits - 1][c].astype(jnp.float32)
            ).astype(jnp.bfloat16)
            span = slice(c * rc, (c + 1) * rc)
            grad_out[span, :] = grad
            first_new, second_new = adam(first[span, :], second[span, :], grad.astype(jnp.float32))
            update = first_new * (1.0 / correct_first) / (
                jnp.sqrt(second_new * (1.0 / correct_second)) + epsilon
            )
            now = current[span, :]
            result = (now - learn_rate * (update + weight_decay * now)).astype(jnp.bfloat16)
            new_weight[span, :] = result
            whole[own] = result
            ag_copy(c, 0).start()
        elif s < 2 * bits:
            ag_copy(c, s - bits - 1).wait_recv()
            ag_copy(c, s - bits).start()
        elif s == 2 * bits:
            ag_copy(c, bits - 1).wait_recv()
            product = jnp.dot(
                whole[c].reshape((n * rc, width)), next_t[...],
                preferred_element_type=jnp.float32,
            )
            product = product.reshape((n, rc, product.shape[1]))
            partial[c] = product

            @pl.when(jnp.logical_not(has_outer))
            def _():
                inward[c] = product.astype(jnp.bfloat16)
                send_inward(c)
        elif s == 2 * bits + 1:
            @pl.when(has_outer)
            def _():
                in_copy(c, False).wait_recv()
                inward[c] = (partial[c] + from_out[c].astype(jnp.float32)).astype(jnp.bfloat16)
                send_inward(c)
        else:
            out_copy(c).wait_recv()

            @pl.when(depth == 0)
            def _():
                next_out[:, c] = (
                    inward[c].astype(jnp.float32) + next_out[:, c].astype(jnp.float32)
                ).astype(jnp.bfloat16)

            @pl.when(has_outer)
            def _():
                out_copy(c).start()

    def own_weight():
        span = window_size(rows)
        start = (me * rows) // 128 * 128
        near = weight[:, pl.ds(pl.multiple_of(start, 128), span)]
        shift = me * rows - start
        row = lax.broadcasted_iota(jnp.int32, (rows, span), 0)
        column = lax.broadcasted_iota(jnp.int32, (rows, span), 1)
        pick = jnp.where(column == row + shift, 1.0, 0.0).astype(jnp.bfloat16)
        current[...] = lax.dot_general(
            pick, near, (((1,), (1,)), ((), ())), preferred_element_type=jnp.float32
        )

    pieces = 3
    cut = width // pieces
    last = 2 * bits + 2
    for t in range(chunks + lag * last):
        for s in reversed(range(last + 1)):
            c = t - lag * s
            if 0 <= c < chunks:
                if s == bits and c == 0:
                    loads[1].wait()
                    loads[2].wait()
                stage(c, s)
        if t == 1:
            loads[0].wait()
            own_weight()
        if t == 2:
            loads[3].wait()
            next_t[...] = next_hidden[...].T
        if t in (4, 6, 8):
            span = slice((t - 4) // 2 * cut, (t - 2) // 2 * cut)
            input_grad[:, span] = lax.dot_general(
                out_grad[...], weight[span, :], (((1,), (1,)), ((), ())),
                preferred_element_type=jnp.float32,
            ).astype(jnp.bfloat16)

    for c in range(chunks):
        for k in range(bits):
            rs_copy(c, k).wait_send()
            ag_copy(c, k).wait_send()
        in_copy(c, False).wait_send()

        @pl.when(has_outer)
        def _():
            out_copy(c).wait_send()


def solution(mesh):
    n, m = mesh.shape["dp"], mesh.shape["tensor"]
    bits = n.bit_length() - 1

    def shards(hidden, out_grad, weight, first_moment, second_moment, next_hidden):
        tokens, width = hidden.shape
        rows = first_moment.shape[0]
        features = out_grad.shape[1]
        rc = 16
        chunks = rows // rc
        cube = (2,) * bits
        vmem = pl.BlockSpec(memory_space=pltpu.VMEM)
        hbm = pl.BlockSpec(memory_space=pl.ANY)
        bf16, f32 = jnp.bfloat16, jnp.float32
        dma = pltpu.SemaphoreType.DMA
        grad, input_grad, new_weight, next_out = pl.pallas_call(
            functools.partial(kernel, n, m, chunks, 3),
            out_shape=(
                jax.ShapeDtypeStruct((rows, width), bf16),
                jax.ShapeDtypeStruct((tokens, width), bf16),
                jax.ShapeDtypeStruct((rows, width), bf16),
                jax.ShapeDtypeStruct((n, chunks, rc, tokens), bf16),
            ),
            in_specs=[vmem] * 2 + [hbm] * 4,
            out_specs=[vmem] * 4,
            scratch_shapes=[
                pltpu.VMEM((features, tokens), bf16),
                pltpu.VMEM(weight.shape, bf16),
                pltpu.VMEM((rows, width), f32),
                pltpu.VMEM((rows, width), f32),
                pltpu.VMEM((rows, width), f32),
                pltpu.VMEM(next_hidden.shape, bf16),
                pltpu.VMEM((width, tokens), bf16),
                pltpu.VMEM((chunks,) + cube + (rc, width), bf16),
                pltpu.VMEM((chunks,) + cube + (rc, width), bf16),
                pltpu.VMEM((chunks, n, rc, tokens), f32),
                pltpu.VMEM((chunks, n, rc, tokens), bf16),
                pltpu.VMEM((chunks, n, rc, tokens), bf16),
            ]
            + [
                pltpu.VMEM((chunks,) + (2,) * (bits - 1 - k) + (rc, width), bf16)
                for k in range(bits)
            ]
            + [
                dma((4,)),
                dma((chunks, bits)), dma((chunks, bits)),
                dma((chunks, bits)), dma((chunks, bits)),
                dma((chunks,)), dma((chunks,)), dma((chunks,)), dma((chunks,)),
            ],
            compiler_params=pltpu.CompilerParams(
                collective_id=0, has_side_effects=True, vmem_limit_bytes=56 * 1024 * 1024
            ),
            cost_estimate=pl.CostEstimate(
                flops=6 * tokens * width * features,
                bytes_accessed=16 * 1024 * 1024,
                transcendentals=rows * width,
            ),
        )(out_grad, hidden, weight, first_moment, second_moment, next_hidden)
        first_new, second_new = adam(first_moment, second_moment, grad.astype(f32))
        next_out = next_out.reshape(features, tokens).T
        return input_grad, first_new, second_new, new_weight, next_out

    placed = (
        P("dp", "tensor"),
        P("dp", None),
        P("tensor", None),
        P("dp", "tensor"),
        P("dp", "tensor"),
        P("dp", "tensor"),
    )
    return jax.shard_map(
        shards,
        mesh=mesh,
        in_specs=placed,
        out_specs=(
            P("dp", "tensor"),
            P("dp", "tensor"),
            P("dp", "tensor"),
            P("dp", "tensor"),
            P("dp", None),
        ),
        check_vma=False,
    )
```
